32 devices in a mesh: groups: 2 (over x), expert: 8 (over z, y), dp: 2 (over core).
Axes of the slice: x: 2, y: 2, z: 4, core: 2. Of those that a mesh axis runs over, the one named last changes fastest.
Arguments:
- tokens: bfloat16 [2048, 7168], P(('groups', 'expert', 'dp')), parts along dimension 0, may hold values from -6 to 6
- expert_ids: int32 [2048, 2], P(('groups', 'expert', 'dp')), parts along dimension 0, may hold values from 0 to 3, all different within a row; in each aligned block of 64 rows (0 to 63, 64 to 127, ...) at most 40 rows name the same one
- router_values: float32 [2048, 2], P(('groups', 'expert', 'dp')), parts along dimension 0, may hold values from 0.1 to 1
- gate_weight: bfloat16 [7168, 4096], P(None, ('expert', 'dp')), may hold values from -0.0625 to 0.0625
- up_weight: bfloat16 [7168, 4096], P(None, ('expert', 'dp')), may hold values from -0.0625 to 0.0625
- down_weight: bfloat16 [4096, 7168], P(('expert', 'dp')), may hold values from -0.1875 to 0.1875
Outputs:
- routed_out: bfloat16 [2048, 7168], P(('groups', 'expert', 'dp')), parts along dimension 0
The draws below stay inside these ranges and needn't reach their ends.
There are 2 independent parts, one for each index of `groups`. The reference program is written for one: setup_inputs(seed, part) draws one part's arguments, and reference() takes and returns one part's arrays. A program takes and returns all parts, laid end to end along the dimension named above; an argument that names none is the same for every part. Nothing has to cross between parts.
Inputs may be any that keep to these rules, and one draw needn't show every extreme that they name: `expert_ids`: each row names 2 different experts. Among the tokens of one device (aligned blocks of 64 rows) no expert is named more than 40 times, and in every draw some expert is named exactly 40 times in some device's tokens.
All inputs are finite; a program needn't handle non-finite values.
Results may differ from the reference program's by a relative error of at most 0.02.
Values may be sent and summed in bfloat16 or wider, within the bound.
No kernel may reach another device: no remote copies, remote signals or barrier semaphores. Data moves between devices by JAX's collectives and lax.ppermute only.
A program may use at most 192 MiB of HBM per device.

```python
import math
import jax
import jax.numpy as jnp
import numpy as np
from jax import lax

D = 7168
FF = 1024
SLICES = 4
FF_DEV = 256
TOK_DEV = 64
EXPERTS = 4
TOP = 2
CAP = 40
TOKENS = 1024


def levels(stream_key, dims, cuts, low, top_value):
    factor_of = 1.0
    for position, blocks in cuts:
        heights = jax.random.uniform(jax.random.fold_in(jax.random.fold_in(stream_key, 6), position), (blocks,), jnp.float32, low / len(cuts), top_value / len(cuts))
        factor_of = factor_of * jnp.repeat(jnp.exp(heights), dims[position] // blocks).reshape((-1,) + (1,) * (len(dims) - 1 - position))
    return factor_of


def shared_out(rng, own, number, rows, count, top, limit, skew):
    sequence = jax.random.permutation(rng, count)
    heavy_load, usual = shares(count, rows * top, limit, skew, True), shares(count, rows * top, limit, skew, False)
    places = jnp.arange(count)

    def named(tallies, offset_by):
        used = int((tallies > 0).sum())
        fixed = max(1, used // 4)
        moved = fixed + (places - fixed + offset_by * (used - fixed)) % max(1, count - fixed)
        return jnp.zeros((count,), jnp.int32).at[sequence[jnp.where(places < fixed, places, moved)]].set(jnp.asarray(tallies, jnp.int32))

    tallies = jnp.where(number % 4 == 0, named(heavy_load, number // 4), named(usual, number - number // 4 - 1))
    mixed = jax.random.permutation(jax.random.fold_in(own, 3), count)
    source_of, sink = mixed[0:count // 2 * 2:2], mixed[1:count // 2 * 2:2]
    room = jnp.minimum(tallies[source_of] - 1, limit - tallies[sink]) // 2
    room = jnp.where((source_of == sequence[0]) | (sink == sequence[0]) | (tallies[sink] == 0), 0, jnp.maximum(room, 0))
    moved = jax.random.randint(jax.random.fold_in(own, 4), (count // 2,), 0, 1 << 20) % (room + 1)
    tallies = tallies.at[source_of].add(-moved).at[sink].add(moved)
    labels = jnp.searchsorted(jnp.cumsum(tallies), jnp.arange(rows * top), side="right").astype(jnp.int32)
    grid = labels.reshape(top, rows).T
    grid = grid[jax.random.permutation(jax.random.fold_in(own, 1), rows)]
    offset_by = jax.random.randint(jax.random.fold_in(own, 2), (rows, 1), 0, top)
    return jnp.take_along_axis(grid, (jnp.arange(top)[None, :] + offset_by) % top, axis=1)


def shares(number_of, total, limit, slope, full):
    loads = [(1 << 20) // math.isqrt(grade ** slope) + 1 for grade in range(1, number_of + 1)]
    largest = limit if full else min(limit, max(-(-total // number_of), total * loads[0] // sum(loads)))
    least = 1 if total - largest >= number_of - 1 else 0
    holding, rest = [largest] + [least] * (number_of - 1), total - largest - least * (number_of - 1)
    while rest > 0:
        candidates = [i for i in range(1, number_of) if holding[i] < largest] or [i for i in range(1, number_of) if holding[i] < limit]
        pool, budget = sum([loads[i] for i in candidates]), rest
        for i in candidates:
            addition = min(limit - holding[i], max(1, budget * loads[i] // pool), rest)
            holding[i] = holding[i] + addition
            rest = rest - addition
    return np.array(holding)


def bell_draw(own_key, shape, spread, bound, cuts=(), kind=jnp.bfloat16):
    gain = levels(own_key, shape, cuts, -0.22, 0.18) if cuts else 1.0
    drawn = jax.random.normal(own_key, shape, jnp.float32) * spread * gain
    return jnp.minimum(jnp.maximum(drawn, -bound), bound).astype(kind)


def setup_inputs(seed: int = 0, part: int = 0) -> dict:
    keys = jax.random.split(jax.random.key(seed), 7)
    own_keys = jax.random.split(jax.random.fold_in(keys[6], part), 7)
    tokens = bell_draw(own_keys[0], (TOKENS, D), 1.0, 6.0, ((0, 16),))
    expert_ids_keys = jax.random.split(jax.random.fold_in(own_keys[1], 1), TOKENS // TOK_DEV)
    expert_ids_turns = jax.random.permutation(jax.random.fold_in(own_keys[1], 3), TOKENS // TOK_DEV)
    expert_ids = jax.vmap(lambda own, number: shared_out(jax.random.fold_in(own_keys[1], 2), own, number, TOK_DEV, EXPERTS, TOP, CAP, 1))(expert_ids_keys, expert_ids_turns).reshape((TOKENS, TOP))
    router_values = jnp.clip(jnp.exp(math.log(1.0) - 2.3025851 * jax.random.uniform(own_keys[2], (TOKENS, TOP), jnp.float32) ** levels(own_keys[2], (TOKENS, TOP), ((0, 16),), -0.2, 0.2)), 0.1, 1.0)
    gate_weight = bell_draw(keys[3], (D, EXPERTS * FF), D ** -0.5, 0.0625, ((1, 16),))
    up_weight = bell_draw(keys[4], (D, EXPERTS * FF), D ** -0.5, 0.0625, ((1, 16),))
    down_weight = bell_draw(keys[5], (EXPERTS * FF, D), FF ** -0.5, 0.1875, ((0, 16),))
    return {"tokens": tokens, "expert_ids": expert_ids, "router_values": router_values, "gate_weight": gate_weight, "up_weight": up_weight, "down_weight": down_weight}


def reference(tokens, expert_ids, router_values, gate_weight, up_weight, down_weight):
    combine = 2.5 * router_values / jnp.sum(router_values, axis=1, keepdims=True)
    blocks = D // 128
    grouped = tokens.astype(jnp.float32).reshape(TOKENS, blocks, 128)
    block_scale = (jnp.max(jnp.abs(grouped), axis=2) / 448.0 + 1e-6).astype(jnp.bfloat16)
    scale_wide = block_scale.astype(jnp.float32)[:, :, None]
    quantized = (grouped / scale_wide).astype(jnp.bfloat16)
    expert_input = (quantized.astype(jnp.float32) * scale_wide).astype(jnp.bfloat16).reshape(TOKENS, D)

    def one_expert(running, expert_index):
        start = (expert_index * FF).astype(jnp.int32)
        gate_cols = lax.dynamic_slice_in_dim(gate_weight, start, FF, 1)
        up_cols = lax.dynamic_slice_in_dim(up_weight, start, FF, 1)
        down_rows = lax.dynamic_slice_in_dim(down_weight, start, FF, 0)
        gate_value = jnp.dot(expert_input, gate_cols, preferred_element_type=jnp.float32)
        up_value = jnp.dot(expert_input, up_cols, preferred_element_type=jnp.float32)
        hidden = (jax.nn.silu(gate_value) * up_value).astype(jnp.bfloat16)
        pieces = jnp.zeros((TOKENS, D), jnp.float32)
        for pair_index in range(SLICES // 2):
            pair_total = jnp.zeros((TOKENS, D), jnp.float32)
            for half in range(2):
                slice_index = 2 * pair_index + half
                lower = slice_index * FF_DEV
                upper = (slice_index + 1) * FF_DEV
                slice_out = jnp.dot(hidden[:, lower:upper], down_rows[lower:upper], preferred_element_type=jnp.float32).astype(jnp.bfloat16)
                slice_out = lax.optimization_barrier(slice_out)
                pair_total = pair_total + slice_out.astype(jnp.float32)
            pair_out = lax.optimization_barrier(pair_total.astype(jnp.bfloat16))
            pieces = pieces + pair_out.astype(jnp.float32)
        weight = jnp.sum(jnp.where(expert_ids == expert_index, combine, jnp.zeros_like(combine)), axis=1)
        return running + weight[:, None] * pieces, None

    running, _ = lax.scan(one_expert, jnp.zeros((TOKENS, D), jnp.float32), jnp.arange(EXPERTS, dtype=jnp.int32))
    return running.astype(jnp.bfloat16)
```

```python
import jax
import jax.numpy as jnp
from jax import lax
from jax.sharding import PartitionSpec as P

SLICES = 4


def expert_rows_of(tokens):
    row_count, feature_width = tokens.shape
    grouped = tokens.astype(jnp.float32).reshape(row_count, feature_width // 128, 128)
    scale = (jnp.max(jnp.abs(grouped), axis=2) / 448.0 + 1e-06).astype(jnp.bfloat16)
    wide = scale.astype(jnp.float32)[:, :, None]
    quantized = (grouped / wide).astype(jnp.bfloat16)
    restored = (quantized.astype(jnp.float32) * wide).astype(jnp.bfloat16)
    return restored.reshape(row_count, feature_width)


def expert_block(rows, gate_weight, up_weight, down_weight):
    gate_value = jnp.dot(rows, gate_weight, preferred_element_type=jnp.float32)
    up_value = jnp.dot(rows, up_weight, preferred_element_type=jnp.float32)
    hidden = (jax.nn.silu(gate_value) * up_value).astype(jnp.bfloat16)
    return jnp.dot(hidden, down_weight, preferred_element_type=jnp.float32).astype(jnp.bfloat16)


def add_rows(left, right):
    return (left.astype(jnp.float32) + right.astype(jnp.float32)).astype(jnp.bfloat16)


def local(tokens, expert_ids, router_values, gate_weight, up_weight, down_weight):
    row_count, _ = tokens.shape
    route_count = expert_ids.shape[1]
    replicas = lax.axis_size("dp")
    chips = lax.axis_size("expert")
    experts = chips * replicas // SLICES
    per = chips // experts
    capacity = row_count * route_count // experts * 5 // 4
    slots = experts * capacity
    assert replicas == 2 and per == 2

    home = lax.axis_index("expert") // per
    across = [(i, i ^ 1) for i in range(chips)]
    cores = [(0, 1), (1, 0)]

    def shifted(step):
        return [(i, (i + per * step) % chips) for i in range(chips)]

    combine = 2.5 * router_values / jnp.sum(router_values, axis=1, keepdims=True)
    chosen = lax.rem(expert_ids - home + experts, experts).reshape(row_count * route_count)
    member = (chosen[:, None] == jnp.arange(experts, dtype=jnp.int32)[None, :]).astype(jnp.int32)
    earlier = jnp.cumsum(member, axis=0) - member
    position = jnp.sum(earlier * member, axis=1)
    slot_index = (chosen * capacity + position).reshape(row_count, route_count)
    pair_table = slot_index[:, :, None] == jnp.arange(slots, dtype=jnp.int32)[None, None, :]
    placer = jnp.any(pair_table, axis=1).astype(jnp.bfloat16)
    weights = jnp.sum(jnp.where(pair_table, combine[:, :, None], 0.0), axis=1)
    weights_high = lax.reduce_precision(weights, 8, 7)
    weights_low = weights - weights_high
    both_weights = jnp.concatenate([weights_high, weights_low], axis=0).astype(jnp.bfloat16)

    rows = expert_rows_of(tokens)
    send = lax.dot_general(
        placer, rows, (((0,), (0,)), ((), ())), preferred_element_type=jnp.float32
    ).astype(jnp.bfloat16)

    returned = []
    for step in range(experts):
        own = send[step * capacity : (step + 1) * capacity]
        if step:
            own = lax.ppermute(own, "expert", shifted(step))
        other = lax.ppermute(own, "expert", across)
        pair = jnp.concatenate([own, other], axis=0)
        far = lax.ppermute(pair, "dp", cores)
        produced = expert_block(
            jnp.concatenate([pair, far], axis=0), gate_weight, up_weight, down_weight
        )
        half = add_rows(
            produced[: 2 * capacity], lax.ppermute(produced[2 * capacity :], "dp", cores)
        )
        whole = add_rows(half[:capacity], lax.ppermute(half[capacity:], "expert", across))
        if step:
            whole = lax.ppermute(whole, "expert", shifted(experts - step))
        returned.append(whole)
    product = jnp.dot(
        both_weights, jnp.concatenate(returned, axis=0), preferred_element_type=jnp.float32
    )
    return (product[:row_count] + product[row_count:]).astype(jnp.bfloat16)


def solution(mesh):
    in_specs = (
        P(("groups", "expert", "dp"), None),
        P(("groups", "expert", "dp"), None),
        P(("groups", "expert", "dp"), None),
        P(None, ("expert", "dp")),
        P(None, ("expert", "dp")),
        P(("expert", "dp"), None),
    )
    out_specs = P(("groups", "expert", "dp"), None)
    return jax.shard_map(local, mesh=mesh, in_specs=in_specs, out_specs=out_specs, check_vma=False)
```

```python
import functools

import jax
import jax.numpy as jnp
from jax import lax
from jax.experimental import pallas as pl
from jax.experimental.pallas import tpu as pltpu
from jax.sharding import PartitionSpec as P

SLICES = 4
SPLIT = True
FIRST = (1, -1)
GATES = {
    "a0": ("b3",),
    "a2": ("o3",),
    "a3": ("b2", "h1",),
    "c2": ("b1",),
    "y3": ("b1",),
    "z2": ("w1",),
    "z3": ("o0", "w2",),
}


FREE = pl.CostEstimate(flops=0, bytes_accessed=0, transcendentals=0)


def pack_kernel(order, home_ref, ids_ref, tokens_ref, *refs):
    piece_refs, rows_ref = refs[:-1], refs[-1]
    experts = len(order)
    capacity = piece_refs[0].shape[0]
    row_count, width = tokens_ref.shape
    for begin in range(0, width, 128):
        block = tokens_ref[:, begin : begin + 128].astype(jnp.float32)
        scale = jnp.max(jnp.abs(block), axis=1, keepdims=True) / 448.0 + 1e-06
        scale = scale.astype(jnp.bfloat16).astype(jnp.float32)
        quantized = (block / scale).astype(jnp.bfloat16).astype(jnp.float32)
        rows_ref[:, begin : begin + 128] = (quantized * scale).astype(jnp.bfloat16)
    distance = ids_ref[...] - home_ref[0]
    distance = jnp.where(distance < 0, distance + experts, distance)
    chunk_of = lax.broadcasted_iota(jnp.int32, (experts, row_count), 0)
    step_of = jnp.zeros_like(chunk_of)
    for k, step in enumerate(order):
        step_of = jnp.where(chunk_of == k, step, step_of)
    member = jnp.zeros((experts, row_count), jnp.float32)
    for route in range(ids_ref.shape[0]):
        member = member + (step_of == distance[route : route + 1]).astype(jnp.float32)
    before = lax.broadcasted_iota(jnp.int32, (row_count, row_count), 0)
    before = before < lax.broadcasted_iota(jnp.int32, (row_count, row_count), 1)
    position = jnp.dot(
        member.astype(jnp.bfloat16),
        before.astype(jnp.float32).astype(jnp.bfloat16),
        preferred_element_type=jnp.float32,
    )
    slot = lax.broadcasted_iota(jnp.int32, (capacity, row_count), 0).astype(jnp.float32)
    columns = width // 4
    for k in range(experts):
        place = jnp.where(slot == position[k : k + 1], member[k : k + 1], 0.0).astype(jnp.bfloat16)
        for begin in range(0, width, columns):
            part = slice(begin, begin + columns)
            picked = jnp.dot(place, rows_ref[:, part], preferred_element_type=jnp.float32)
            piece_refs[k][:, part] = picked.astype(jnp.bfloat16)


def packed(tokens, expert_ids, home, order, capacity):
    shape = jax.ShapeDtypeStruct((capacity, tokens.shape[1]), jnp.bfloat16)
    vmem = pl.BlockSpec(memory_space=pltpu.VMEM)
    return pl.pallas_call(
        functools.partial(pack_kernel, order),
        in_specs=[pl.BlockSpec(memory_space=pltpu.SMEM), vmem, vmem],
        out_specs=[vmem] * len(order),
        out_shape=[shape] * len(order),
        scratch_shapes=[pltpu.VMEM(tokens.shape, jnp.bfloat16)],
        compiler_params=pltpu.CompilerParams(vmem_limit_bytes=24 << 20),
    )(home.reshape(1), expert_ids.T, tokens)


def hidden_kernel(steps, rows_ref, gate_ref, up_ref, hidden_ref, gate_sum, up_sum):
    step = pl.program_id(0)
    rows = rows_ref[...]
    gate = jnp.dot(rows, gate_ref[...], preferred_element_type=jnp.float32)
    up = jnp.dot(rows, up_ref[...], preferred_element_type=jnp.float32)

    @pl.when(step == 0)
    def _():
        gate_sum[...] = gate
        up_sum[...] = up

    @pl.when(step > 0)
    def _():
        gate_sum[...] += gate
        up_sum[...] += up

    @pl.when(step == steps - 1)
    def _():
        value = gate_sum[...]
        hidden_ref[...] = (value / (1.0 + jnp.exp(-value)) * up_sum[...]).astype(jnp.bfloat16)


def hidden_of(rows, gate_weight, up_weight, steps=4):
    count, width = rows.shape
    units = gate_weight.shape[1]
    depth = width // steps
    return pl.pallas_call(
        functools.partial(hidden_kernel, steps),
        grid=(steps,),
        in_specs=[
            pl.BlockSpec((count, depth), lambda i: (0, i)),
            pl.BlockSpec((depth, units), lambda i: (i, 0)),
            pl.BlockSpec((depth, units), lambda i: (i, 0)),
        ],
        out_specs=pl.BlockSpec((count, units), lambda i: (0, 0)),
        out_shape=jax.ShapeDtypeStruct((count, units), jnp.bfloat16),
        scratch_shapes=[pltpu.VMEM((count, units), jnp.float32)] * 2,
        compiler_params=pltpu.CompilerParams(vmem_limit_bytes=16 << 20),
        cost_estimate=FREE,
    )(rows, gate_weight, up_weight)


def down_kernel(hidden_ref, down_ref, near_ref, away_ref):
    made = jnp.dot(hidden_ref[...], down_ref[...], preferred_element_type=jnp.float32)
    half = near_ref.shape[0]
    near_ref[...] = made[:half].astype(jnp.bfloat16)
    away_ref[...] = made[half:].astype(jnp.bfloat16)


def outputs_of(hidden, down_weight, steps=2):
    count, units = hidden.shape
    width = down_weight.shape[1]
    columns = width // steps
    return pl.pallas_call(
        down_kernel,
        grid=(steps,),
        in_specs=[
            pl.BlockSpec((count, units), lambda i: (0, 0)),
            pl.BlockSpec((units, columns), lambda i: (0, i)),
        ],
        out_specs=[pl.BlockSpec((count // 2, columns), lambda i: (0, i))] * 2,
        out_shape=[jax.ShapeDtypeStruct((count // 2, width), jnp.bfloat16)] * 2,
        compiler_params=pltpu.CompilerParams(vmem_limit_bytes=16 << 20),
        cost_estimate=FREE,
    )(hidden, down_weight)


def no_rows(width, *earlier):
    zero = jnp.zeros((1, width), jnp.float32)
    for rows in earlier:
        row = rows[:1].astype(jnp.float32) * 0.0
        if row.shape[1] < width:
            row = jnp.concatenate([row] * (width // row.shape[1]), axis=1)
        zero = zero + row[:, :width]
    return zero


def hold(rows, *earlier):
    return (rows.astype(jnp.float32) + no_rows(rows.shape[1], *earlier)).astype(jnp.bfloat16)


def add_rows(left, right):
    return (left.astype(jnp.float32) + right.astype(jnp.float32)).astype(jnp.bfloat16)


def local(tokens, expert_ids, router_values, gate_weight, up_weight, down_weight):
    row_count, width = tokens.shape
    route_count = expert_ids.shape[1]
    replicas = lax.axis_size("dp")
    chips = lax.axis_size("expert")
    experts = chips * replicas // SLICES
    per = chips // experts
    capacity = row_count * route_count // experts * 5 // 4
    assert replicas == 2 and per == 2 and experts >= 4
    wide = width // 2

    home = lax.axis_index("expert") // per
    core = lax.axis_index("dp")
    across = [(i, i ^ 1) for i in range(chips)]

    def along(rows, step):
        return lax.ppermute(
            rows, "expert", [(i, (i + per * step) % chips) for i in range(chips)]
        )

    def over(rows):
        return lax.ppermute(rows, "expert", across)

    def swap(rows):
        return lax.ppermute(rows, "dp", [(0, 1), (1, 0)])

    order = [0] + [step % experts for step in FIRST]
    order += [step for step in range(experts) if step not in order]
    last = experts - 1

    combine = 2.5 * router_values / jnp.sum(router_values, axis=1, keepdims=True)
    distance = lax.rem(expert_ids - home + experts, experts)
    chosen = jnp.zeros_like(distance)
    for k, step in enumerate(order):
        chosen = jnp.where(distance == step, k, chosen)
    chosen = chosen.reshape(row_count * route_count)
    member = (chosen[:, None] == jnp.arange(experts, dtype=jnp.int32)[None, :]).astype(jnp.int32)
    earlier_rows = jnp.cumsum(member, axis=0) - member
    position = jnp.sum(earlier_rows * member, axis=1)
    slot_index = (chosen * (2 * capacity) + position).reshape(row_count, route_count)
    slots = jnp.arange(experts * 2 * capacity, dtype=jnp.int32)
    pair_table = slot_index[:, :, None] == slots[None, None, :]
    weights = jnp.sum(jnp.where(pair_table, combine[:, :, None], 0.0), axis=1)
    weights_high = lax.reduce_precision(weights, 8, 7)
    weights_low = weights - weights_high
    my_weights = jnp.concatenate([weights_high, weights_low], axis=0).astype(jnp.bfloat16)
    peer_weights = swap(my_weights)
    peer_weights = jnp.concatenate(
        [jnp.zeros((2 * row_count, capacity), jnp.bfloat16), peer_weights[:, :-capacity]], axis=1
    )
    all_weights = jnp.concatenate([my_weights, peer_weights], axis=0)

    down_far = swap(lax.dynamic_slice_in_dim(down_weight, (1 - core) * wide, wide, 1))
    down_near = lax.dynamic_slice_in_dim(down_weight, core * wide, wide, 1)
    down_half = jnp.concatenate([down_near, down_far], axis=0)

    pieces = packed(tokens, expert_ids, home, tuple(order), capacity)

    def piece(k, low, high, *earlier):
        part = pieces[k] if high - low == capacity else pieces[k][low:high]
        return hold(part, *earlier) if earlier else part

    seen = {}

    def gates(point):
        return [seen[name] for name in GATES.get(point, ()) if name in seen]

    def maybe_hold(rows, point):
        found = gates(point)
        return hold(rows, *found) if found else rows

    own, own_far, near, raw = {}, {}, {}, {}

    def dispatch(k):
        if k == 0:
            own[k] = piece(k, 0, capacity)
        elif order[k] == 2 and SPLIT:
            half = (capacity // 2 + 7) // 8 * 8
            upper = along(piece(k, 0, half, *gates("z%d" % k)), order[k])
            seen["u3"] = upper
            lower = along(piece(k, half, capacity, upper, *gates("z%db" % k)), order[k])
            own[k] = jnp.concatenate([upper, lower], axis=0)
        else:
            own[k] = along(piece(k, 0, capacity, *gates("z%d" % k)), order[k])
        seen["w%d" % k] = own[k]

    def spread(k):
        own[k] = maybe_hold(own[k], "y%d" % k)
        own_far[k] = swap(own[k])
        seen["o%d" % k] = over(own[k])

    def turned(hidden):
        quarters = [hidden[i * capacity : (i + 1) * capacity] for i in range(4)]
        return jnp.concatenate([quarters[i] for i in (1, 0, 3, 2)], axis=0)

    def compute(k):
        other = maybe_hold(seen["o%d" % k], "c%d" % k)
        flat = jnp.concatenate([own[k], own_far[k], other, swap(other)], axis=0)
        hidden = hidden_of(flat, gate_weight, up_weight)
        hidden = jnp.concatenate([hidden, turned(swap(hidden))], axis=1)
        near[k], raw[k] = outputs_of(hidden, down_half)
        seen["n%d" % k] = near[k]

    def merge(k):
        seen["b%d" % k] = over(maybe_hold(raw[k], "a%d" % k))

    def give_back(k):
        total = add_rows(near[k], seen["b%d" % k])
        seen["h%d" % k] = along(total, -order[k]) if k else total

    for k in range(3):
        dispatch(k)
        spread(k)
    dispatch(3)
    compute(1)
    for k in range(2, last):
        merge(k - 1)
        compute(k)
        spread(k + 1)
        give_back(k - 1)
        if k + 2 < experts:
            dispatch(k + 2)
    compute(0)
    merge(last - 1)
    compute(last)
    merge(last)
    give_back(last - 1)
    merge(0)
    give_back(last)
    give_back(0)
    whole = [seen["h%d" % k] for k in range(experts)]
    returned = jnp.concatenate(whole, axis=0)
    product = jnp.dot(all_weights, returned, preferred_element_type=jnp.float32)
    product = product.reshape(2, 2, row_count, wide)
    halves = (product[:, 0] + product[:, 1]).astype(jnp.bfloat16)
    mine, got = halves[0], swap(halves[1])
    return jnp.where(
        core == 0,
        jnp.concatenate([mine, got], axis=1),
        jnp.concatenate([got, mine], axis=1),
    )


def solution(mesh):
    in_specs = (
        P(("groups", "expert", "dp"), None),
        P(("groups", "expert", "dp"), None),
        P(("groups", "expert", "dp"), None),
        P(None, ("expert", "dp")),
        P(None, ("expert", "dp")),
        P(("expert", "dp"), None),
    )
    out_specs = P(("groups", "expert", "dp"), None)
    return jax.shard_map(local, mesh=mesh, in_specs=in_specs, out_specs=out_specs, check_vma=False)
```

```python
import functools

import jax
import jax.numpy as jnp
from jax import lax
from jax.experimental import pallas as pl
from jax.experimental.pallas import tpu as pltpu
from jax.sharding import PartitionSpec as P

SLICES = 4
SPLIT = False
HALVED = ()
FIRST = (1, -1)
GATES = {
    "a0": ("b1",),
    "a2": ("n0",),
    "a3": ("h1",),
    "c3": ("b1",),
    "h3": ("b2", "h2",),
    "y3": ("b1",),
    "z2": ("w1",),
    "z3": ("w2",),
}


FREE = pl.CostEstimate(flops=0, bytes_accessed=0, transcendentals=0)


def pack_kernel(order, home_ref, ids_ref, tokens_ref, *refs):
    piece_refs, rows_ref = refs[:-1], refs[-1]
    experts = len(order)
    capacity = piece_refs[0].shape[0]
    row_count, width = tokens_ref.shape
    for begin in range(0, width, 128):
        block = tokens_ref[:, begin : begin + 128].astype(jnp.float32)
        scale = jnp.max(jnp.abs(block), axis=1, keepdims=True) / 448.0 + 1e-06
        scale = scale.astype(jnp.bfloat16).astype(jnp.float32)
        quantized = (block / scale).astype(jnp.bfloat16).astype(jnp.float32)
        rows_ref[:, begin : begin + 128] = (quantized * scale).astype(jnp.bfloat16)
    distance = ids_ref[...] - home_ref[0]
    distance = jnp.where(distance < 0, distance + experts, distance)
    chunk_of = lax.broadcasted_iota(jnp.int32, (experts, row_count), 0)
    step_of = jnp.zeros_like(chunk_of)
    for k, step in enumerate(order):
        step_of = jnp.where(chunk_of == k, step, step_of)
    member = jnp.zeros((experts, row_count), jnp.float32)
    for route in range(ids_ref.shape[0]):
        member = member + (step_of == distance[route : route + 1]).astype(jnp.float32)
    before = lax.broadcasted_iota(jnp.int32, (row_count, row_count), 0)
    before = before < lax.broadcasted_iota(jnp.int32, (row_count, row_count), 1)
    position = jnp.dot(
        member.astype(jnp.bfloat16),
        before.astype(jnp.float32).astype(jnp.bfloat16),
        preferred_element_type=jnp.float32,
    )
    slot = lax.broadcasted_iota(jnp.int32, (capacity, row_count), 0).astype(jnp.float32)
    columns = width // 4
    for k in range(experts):
        place = jnp.where(slot == position[k : k + 1], member[k : k + 1], 0.0).astype(jnp.bfloat16)
        for begin in range(0, width, columns):
            part = slice(begin, begin + columns)
            picked = jnp.dot(place, rows_ref[:, part], preferred_element_type=jnp.float32)
            piece_refs[k][:, part] = picked.astype(jnp.bfloat16)


def packed(tokens, expert_ids, home, order, capacity):
    shape = jax.ShapeDtypeStruct((capacity, tokens.shape[1]), jnp.bfloat16)
    vmem = pl.BlockSpec(memory_space=pltpu.VMEM)
    return pl.pallas_call(
        functools.partial(pack_kernel, order),
        in_specs=[pl.BlockSpec(memory_space=pltpu.SMEM), vmem, vmem],
        out_specs=[vmem] * len(order),
        out_shape=[shape] * len(order),
        scratch_shapes=[pltpu.VMEM(tokens.shape, jnp.bfloat16)],
        compiler_params=pltpu.CompilerParams(vmem_limit_bytes=24 << 20),
    )(home.reshape(1), expert_ids.T, tokens)


def hidden_kernel(rows_ref, gate_ref, up_ref, hidden_ref):
    rows = rows_ref[...]
    gate = jnp.dot(rows, gate_ref[...], preferred_element_type=jnp.float32)
    up = jnp.dot(rows, up_ref[...], preferred_element_type=jnp.float32)
    hidden_ref[...] = (gate / (1.0 + jnp.exp(-gate)) * up).astype(jnp.bfloat16)


def hidden_of(rows, gate_weight, up_weight):
    vmem = pl.BlockSpec(memory_space=pltpu.VMEM)
    return pl.pallas_call(
        hidden_kernel,
        in_specs=[vmem] * 3,
        out_specs=vmem,
        out_shape=jax.ShapeDtypeStruct((rows.shape[0], gate_weight.shape[1]), jnp.bfloat16),
        compiler_params=pltpu.CompilerParams(vmem_limit_bytes=24 << 20),
        cost_estimate=FREE,
    )(rows, gate_weight, up_weight)


def down_kernel(hidden_ref, down_ref, *made_refs):
    made = jnp.dot(hidden_ref[...], down_ref[...], preferred_element_type=jnp.float32)
    begin = 0
    for made_ref in made_refs:
        count = made_ref.shape[0]
        made_ref[...] = made[begin : begin + count].astype(jnp.bfloat16)
        begin += count


def outputs_of(hidden, down_weight, counts):
    vmem = pl.BlockSpec(memory_space=pltpu.VMEM)
    width = down_weight.shape[1]
    return pl.pallas_call(
        down_kernel,
        in_specs=[vmem] * 2,
        out_specs=[vmem] * len(counts),
        out_shape=[jax.ShapeDtypeStruct((n, width), jnp.bfloat16) for n in counts],
        compiler_params=pltpu.CompilerParams(vmem_limit_bytes=24 << 20),
        cost_estimate=FREE,
    )(hidden, down_weight)


def no_rows(width, *earlier):
    zero = jnp.zeros((1, width), jnp.float32)
    for rows in earlier:
        row = rows[:1].astype(jnp.float32) * 0.0
        if row.shape[1] < width:
            row = jnp.concatenate([row] * (width // row.shape[1]), axis=1)
        zero = zero + row[:, :width]
    return zero


def hold(rows, *earlier):
    return (rows.astype(jnp.float32) + no_rows(rows.shape[1], *earlier)).astype(jnp.bfloat16)


def add_rows(left, right):
    return (left.astype(jnp.float32) + right.astype(jnp.float32)).astype(jnp.bfloat16)


def local(tokens, expert_ids, router_values, gate_weight, up_weight, down_weight):
    row_count, width = tokens.shape
    route_count = expert_ids.shape[1]
    replicas = lax.axis_size("dp")
    chips = lax.axis_size("expert")
    experts = chips * replicas // SLICES
    per = chips // experts
    capacity = row_count * route_count // experts * 5 // 4
    assert replicas == 2 and per == 2 and experts >= 4
    wide = width // 2

    home = lax.axis_index("expert") // per
    core = lax.axis_index("dp")
    across = [(i, i ^ 1) for i in range(chips)]

    def along(rows, step):
        return lax.ppermute(
            rows, "expert", [(i, (i + per * step) % chips) for i in range(chips)]
        )

    def over(rows):
        return lax.ppermute(rows, "expert", across)

    def swap(rows):
        return lax.ppermute(rows, "dp", [(0, 1), (1, 0)])

    order = [0] + [step % experts for step in FIRST]
    order += [step for step in range(experts) if step not in order]
    last = experts - 1

    combine = 2.5 * router_values / jnp.sum(router_values, axis=1, keepdims=True)
    distance = lax.rem(expert_ids - home + experts, experts)
    chosen = jnp.zeros_like(distance)
    for k, step in enumerate(order):
        chosen = jnp.where(distance == step, k, chosen)
    chosen = chosen.reshape(row_count * route_count)
    member = (chosen[:, None] == jnp.arange(experts, dtype=jnp.int32)[None, :]).astype(jnp.int32)
    earlier_rows = jnp.cumsum(member, axis=0) - member
    position = jnp.sum(earlier_rows * member, axis=1)
    slot_index = (chosen * (2 * capacity) + position).reshape(row_count, route_count)
    slots = jnp.arange(experts * 2 * capacity, dtype=jnp.int32)
    pair_table = slot_index[:, :, None] == slots[None, None, :]
    weights = jnp.sum(jnp.where(pair_table, combine[:, :, None], 0.0), axis=1)
    weights_high = lax.reduce_precision(weights, 8, 7)
    weights_low = weights - weights_high
    my_weights = jnp.concatenate([weights_high, weights_low], axis=0).astype(jnp.bfloat16)
    peer_weights = swap(my_weights)
    peer_weights = jnp.concatenate(
        [jnp.zeros((2 * row_count, capacity), jnp.bfloat16), peer_weights[:, :-capacity]], axis=1
    )
    all_weights = jnp.concatenate([my_weights, peer_weights], axis=0)

    down_far = swap(lax.dynamic_slice_in_dim(down_weight, (1 - core) * wide, wide, 1))
    down_near = lax.dynamic_slice_in_dim(down_weight, core * wide, wide, 1)
    down_half = jnp.concatenate([down_near, down_far], axis=0)

    pieces = packed(tokens, expert_ids, home, tuple(order), capacity)

    def piece(k, low, high, *earlier):
        part = pieces[k] if high - low == capacity else pieces[k][low:high]
        return hold(part, *earlier) if earlier else part

    seen = {}

    def gates(point):
        return [seen[name] for name in GATES.get(point, ()) if name in seen]

    def maybe_hold(rows, point):
        found = gates(point)
        return hold(rows, *found) if found else rows

    own, own_far, near, raw, back, whole = {}, {}, {}, {}, {}, []

    def dispatch(k):
        if k == 0:
            own[k] = piece(k, 0, capacity)
        elif order[k] == 2 and SPLIT:
            half = (capacity // 2 + 7) // 8 * 8
            upper = along(piece(k, 0, half, *gates("z%d" % k)), order[k])
            seen["u3"] = upper
            lower = along(piece(k, half, capacity, upper, *gates("z%db" % k)), order[k])
            own[k] = jnp.concatenate([upper, lower], axis=0)
        else:
            own[k] = along(piece(k, 0, capacity, *gates("z%d" % k)), order[k])
        seen["w%d" % k] = own[k]

    def spread(k):
        own[k] = maybe_hold(own[k], "y%d" % k)
        own_far[k] = swap(own[k])
        seen["o%d" % k] = over(own[k])

    def turned(hidden):
        quarters = [hidden[i * capacity : (i + 1) * capacity] for i in range(4)]
        return jnp.concatenate([quarters[i] for i in (1, 0, 3, 2)], axis=0)

    def compute(k):
        other = maybe_hold(seen["o%d" % k], "c%d" % k)
        flat = jnp.concatenate([own[k], own_far[k], other, swap(other)], axis=0)
        hidden = hidden_of(flat, gate_weight, up_weight)
        hidden = jnp.concatenate([hidden, turned(swap(hidden))], axis=1)
        parts = 2 if k in HALVED else 1
        made = outputs_of(hidden, down_half, [2 * capacity // parts] * (2 * parts))
        near[k], raw[k] = made[:parts], made[parts:]
        seen["n%d" % k] = near[k][0]

    def merge(k):
        back[k] = [over(maybe_hold(rows, "a%d" % k)) for rows in raw[k]]
        seen["b%d" % k] = back[k][-1]
        seen["B%d" % k] = back[k][0]

    def give_back(k):
        totals = [add_rows(*pair) for pair in zip(near[k], back[k])]
        if k:
            totals = [along(maybe_hold(rows, "h%d" % k), -order[k]) for rows in totals]
        seen["h%d" % k] = totals[-1]
        whole.extend(zip([2 * k, 2 * k + 1], totals))

    for k in range(3):
        dispatch(k)
        spread(k)
    dispatch(3)
    compute(1)
    for k in range(2, last):
        merge(k - 1)
        compute(k)
        spread(k + 1)
        give_back(k - 1)
        if k + 2 < experts:
            dispatch(k + 2)
    compute(0)
    merge(last - 1)
    compute(last)
    merge(last)
    give_back(last - 1)
    merge(0)
    give_back(last)
    give_back(0)
    whole = [rows for _, rows in sorted(whole, key=lambda item: item[0])]
    returned = jnp.concatenate(whole, axis=0)
    product = jnp.dot(all_weights, returned, preferred_element_type=jnp.float32)
    product = product.reshape(2, 2, row_count, wide)
    halves = (product[:, 0] + product[:, 1]).astype(jnp.bfloat16)
    mine, got = halves[0], swap(halves[1])
    return jnp.where(
        core == 0,
        jnp.concatenate([mine, got], axis=1),
        jnp.concatenate([got, mine], axis=1),
    )


def solution(mesh):
    in_specs = (
        P(("groups", "expert", "dp"), None),
        P(("groups", "expert", "dp"), None),
        P(("groups", "expert", "dp"), None),
        P(None, ("expert", "dp")),
        P(None, ("expert", "dp")),
        P(("expert", "dp"), None),
    )
    out_specs = P(("groups", "expert", "dp"), None)
    return jax.shard_map(local, mesh=mesh, in_specs=in_specs, out_specs=out_specs, check_vma=False)
```

```python
import functools

import jax
import jax.numpy as jnp
from jax import lax
from jax.experimental import pallas as pl
from jax.experimental.pallas import tpu as pltpu
from jax.sharding import PartitionSpec as P

SLICES = 4
SPLIT = False
HALVED = ()
FIRST = (1, -1)
GATES = {
    "a2": ("n0",),
    "a3": ("h1",),
    "c2": ("n1",),
    "c3": ("b1",),
    "h3": ("h2",),
    "y3": ("b1",),
    "z2": ("o0", "w1",),
    "z3": ("w2",),
}


FREE = pl.CostEstimate(flops=0, bytes_accessed=0, transcendentals=0)


def pack_kernel(order, home_ref, ids_ref, tokens_ref, *refs):
    piece_refs, rows_ref = refs[:-1], refs[-1]
    experts = len(order)
    capacity = piece_refs[0].shape[0]
    row_count, width = tokens_ref.shape
    for begin in range(0, width, 128):
        block = tokens_ref[:, begin : begin + 128].astype(jnp.float32)
        scale = jnp.max(jnp.abs(block), axis=1, keepdims=True) / 448.0 + 1e-06
        scale = scale.astype(jnp.bfloat16).astype(jnp.float32)
        quantized = (block / scale).astype(jnp.bfloat16).astype(jnp.float32)
        rows_ref[:, begin : begin + 128] = (quantized * scale).astype(jnp.bfloat16)
    distance = ids_ref[...] - home_ref[0]
    distance = jnp.where(distance < 0, distance + experts, distance)
    chunk_of = lax.broadcasted_iota(jnp.int32, (experts, row_count), 0)
    step_of = jnp.zeros_like(chunk_of)
    for k, step in enumerate(order):
        step_of = jnp.where(chunk_of == k, step, step_of)
    member = jnp.zeros((experts, row_count), jnp.float32)
    for route in range(ids_ref.shape[0]):
        member = member + (step_of == distance[route : route + 1]).astype(jnp.float32)
    before = lax.broadcasted_iota(jnp.int32, (row_count, row_count), 0)
    before = before < lax.broadcasted_iota(jnp.int32, (row_count, row_count), 1)
    position = jnp.dot(
        member.astype(jnp.bfloat16),
        before.astype(jnp.float32).astype(jnp.bfloat16),
        preferred_element_type=jnp.float32,
    )
    slot = lax.broadcasted_iota(jnp.int32, (capacity, row_count), 0).astype(jnp.float32)
    columns = width // 4
    for k in range(experts):
        place = jnp.where(slot == position[k : k + 1], member[k : k + 1], 0.0).astype(jnp.bfloat16)
        for begin in range(0, width, columns):
            part = slice(begin, begin + columns)
            picked = jnp.dot(place, rows_ref[:, part], preferred_element_type=jnp.float32)
            piece_refs[k][:, part] = picked.astype(jnp.bfloat16)


def packed(tokens, expert_ids, home, order, capacity):
    shape = jax.ShapeDtypeStruct((capacity, tokens.shape[1]), jnp.bfloat16)
    vmem = pl.BlockSpec(memory_space=pltpu.VMEM)
    return pl.pallas_call(
        functools.partial(pack_kernel, order),
        in_specs=[pl.BlockSpec(memory_space=pltpu.SMEM), vmem, vmem],
        out_specs=[vmem] * len(order),
        out_shape=[shape] * len(order),
        scratch_shapes=[pltpu.VMEM(tokens.shape, jnp.bfloat16)],
        compiler_params=pltpu.CompilerParams(vmem_limit_bytes=24 << 20),
    )(home.reshape(1), expert_ids.T, tokens)


def hidden_kernel(rows_ref, gate_ref, up_ref, hidden_ref):
    rows = rows_ref[...]
    gate = jnp.dot(rows, gate_ref[...], preferred_element_type=jnp.float32)
    up = jnp.dot(rows, up_ref[...], preferred_element_type=jnp.float32)
    hidden_ref[...] = (gate / (1.0 + jnp.exp(-gate)) * up).astype(jnp.bfloat16)


def hidden_of(rows, gate_weight, up_weight):
    vmem = pl.BlockSpec(memory_space=pltpu.VMEM)
    return pl.pallas_call(
        hidden_kernel,
        in_specs=[vmem] * 3,
        out_specs=vmem,
        out_shape=jax.ShapeDtypeStruct((rows.shape[0], gate_weight.shape[1]), jnp.bfloat16),
        compiler_params=pltpu.CompilerParams(vmem_limit_bytes=24 << 20),
        cost_estimate=FREE,
    )(rows, gate_weight, up_weight)


def down_kernel(hidden_ref, down_ref, *made_refs):
    made = jnp.dot(hidden_ref[...], down_ref[...], preferred_element_type=jnp.float32)
    begin = 0
    for made_ref in made_refs:
        count = made_ref.shape[0]
        made_ref[...] = made[begin : begin + count].astype(jnp.bfloat16)
        begin += count


def outputs_of(hidden, down_weight, counts):
    vmem = pl.BlockSpec(memory_space=pltpu.VMEM)
    width = down_weight.shape[1]
    return pl.pallas_call(
        down_kernel,
        in_specs=[vmem] * 2,
        out_specs=[vmem] * len(counts),
        out_shape=[jax.ShapeDtypeStruct((n, width), jnp.bfloat16) for n in counts],
        compiler_params=pltpu.CompilerParams(vmem_limit_bytes=24 << 20),
        cost_estimate=FREE,
    )(hidden, down_weight)


def no_rows(width, *earlier):
    zero = jnp.zeros((1, width), jnp.float32)
    for rows in earlier:
        row = rows[:1].astype(jnp.float32) * 0.0
        if row.shape[1] < width:
            row = jnp.concatenate([row] * (width // row.shape[1]), axis=1)
        zero = zero + row[:, :width]
    return zero


def hold(rows, *earlier):
    return (rows.astype(jnp.float32) + no_rows(rows.shape[1], *earlier)).astype(jnp.bfloat16)


def add_rows(left, right):
    return (left.astype(jnp.float32) + right.astype(jnp.float32)).astype(jnp.bfloat16)


def local(tokens, expert_ids, router_values, gate_weight, up_weight, down_weight):
    row_count, width = tokens.shape
    route_count = expert_ids.shape[1]
    replicas = lax.axis_size("dp")
    chips = lax.axis_size("expert")
    experts = chips * replicas // SLICES
    per = chips // experts
    capacity = row_count * route_count // experts * 5 // 4
    assert replicas == 2 and per == 2 and experts >= 4
    wide = width // 2

    home = lax.axis_index("expert") // per
    core = lax.axis_index("dp")
    across = [(i, i ^ 1) for i in range(chips)]

    def along(rows, step):
        return lax.ppermute(
            rows, "expert", [(i, (i + per * step) % chips) for i in range(chips)]
        )

    def over(rows):
        return lax.ppermute(rows, "expert", across)

    def swap(rows):
        return lax.ppermute(rows, "dp", [(0, 1), (1, 0)])

    order = [0] + [step % experts for step in FIRST]
    order += [step for step in range(experts) if step not in order]
    last = experts - 1

    combine = 2.5 * router_values / jnp.sum(router_values, axis=1, keepdims=True)
    distance = lax.rem(expert_ids - home + experts, experts)
    chosen = jnp.zeros_like(distance)
    for k, step in enumerate(order):
        chosen = jnp.where(distance == step, k, chosen)
    chosen = chosen.reshape(row_count * route_count)
    member = (chosen[:, None] == jnp.arange(experts, dtype=jnp.int32)[None, :]).astype(jnp.int32)
    earlier_rows = jnp.cumsum(member, axis=0) - member
    position = jnp.sum(earlier_rows * member, axis=1)
    slot_index = (chosen * (2 * capacity) + position).reshape(row_count, route_count)
    slots = jnp.arange(experts * 2 * capacity, dtype=jnp.int32)
    pair_table = slot_index[:, :, None] == slots[None, None, :]
    weights = jnp.sum(jnp.where(pair_table, combine[:, :, None], 0.0), axis=1)
    weights_high = lax.reduce_precision(weights, 8, 7)
    weights_low = weights - weights_high
    my_weights = jnp.concatenate([weights_high, weights_low], axis=0).astype(jnp.bfloat16)
    peer_weights = swap(my_weights)
    peer_weights = jnp.concatenate(
        [jnp.zeros((2 * row_count, capacity), jnp.bfloat16), peer_weights[:, :-capacity]], axis=1
    )
    all_weights = jnp.concatenate([my_weights, peer_weights], axis=0)

    down_far = swap(lax.dynamic_slice_in_dim(down_weight, (1 - core) * wide, wide, 1))
    down_near = lax.dynamic_slice_in_dim(down_weight, core * wide, wide, 1)
    down_half = jnp.concatenate([down_near, down_far], axis=0)

    pieces = packed(tokens, expert_ids, home, tuple(order), capacity)

    def piece(k, low, high, *earlier):
        part = pieces[k] if high - low == capacity else pieces[k][low:high]
        return hold(part, *earlier) if earlier else part

    seen = {}

    def gates(point):
        return [seen[name] for name in GATES.get(point, ()) if name in seen]

    def maybe_hold(rows, point):
        found = gates(point)
        return hold(rows, *found) if found else rows

    own, own_far, near, raw, back, whole = {}, {}, {}, {}, {}, []

    def dispatch(k):
        if k == 0:
            own[k] = piece(k, 0, capacity)
        elif order[k] == 2 and SPLIT:
            half = (capacity // 2 + 7) // 8 * 8
            upper = along(piece(k, 0, half, *gates("z%d" % k)), order[k])
            seen["u3"] = upper
            lower = along(piece(k, half, capacity, upper, *gates("z%db" % k)), order[k])
            own[k] = jnp.concatenate([upper, lower], axis=0)
        else:
            own[k] = along(piece(k, 0, capacity, *gates("z%d" % k)), order[k])
        seen["w%d" % k] = own[k]

    def spread(k):
        own[k] = maybe_hold(own[k], "y%d" % k)
        own_far[k] = swap(own[k])
        seen["o%d" % k] = over(own[k])

    def turned(hidden):
        quarters = [hidden[i * capacity : (i + 1) * capacity] for i in range(4)]
        return jnp.concatenate([quarters[i] for i in (1, 0, 3, 2)], axis=0)

    def compute(k):
        other = maybe_hold(seen["o%d" % k], "c%d" % k)
        flat = jnp.concatenate([own[k], own_far[k], other, swap(other)], axis=0)
        hidden = hidden_of(flat, gate_weight, up_weight)
        hidden = jnp.concatenate([hidden, turned(swap(hidden))], axis=1)
        parts = 2 if k in HALVED else 1
        made = outputs_of(hidden, down_half, [2 * capacity // parts] * (2 * parts))
        near[k], raw[k] = made[:parts], made[parts:]
        seen["n%d" % k] = near[k][0]

    def merge(k):
        back[k] = [over(maybe_hold(rows, "a%d" % k)) for rows in raw[k]]
        seen["b%d" % k] = back[k][-1]
        seen["B%d" % k] = back[k][0]

    def give_back(k):
        totals = [add_rows(*pair) for pair in zip(near[k], back[k])]
        if k:
            totals = [along(maybe_hold(rows, "h%d" % k), -order[k]) for rows in totals]
        seen["h%d" % k] = totals[-1]
        whole.extend(zip([2 * k, 2 * k + 1], totals))

    for k in range(3):
        dispatch(k)
        spread(k)
    dispatch(3)
    compute(1)
    for k in range(2, last):
        merge(k - 1)
        compute(k)
        spread(k + 1)
        give_back(k - 1)
        if k + 2 < experts:
            dispatch(k + 2)
    compute(0)
    merge(last - 1)
    compute(last)
    merge(last)
    give_back(last - 1)
    merge(0)
    give_back(last)
    give_back(0)
    whole = [rows for _, rows in sorted(whole, key=lambda item: item[0])]
    returned = jnp.concatenate(whole, axis=0)
    product = jnp.dot(all_weights, returned, preferred_element_type=jnp.float32)
    product = product.reshape(2, 2, row_count, wide)
    halves = (product[:, 0] + product[:, 1]).astype(jnp.bfloat16)
    mine, got = halves[0], swap(halves[1])
    return jnp.where(
        core == 0,
        jnp.concatenate([mine, got], axis=1),
        jnp.concatenate([got, mine], axis=1),
    )


def solution(mesh):
    in_specs = (
        P(("groups", "expert", "dp"), None),
        P(("groups", "expert", "dp"), None),
        P(("groups", "expert", "dp"), None),
        P(None, ("expert", "dp")),
        P(None, ("expert", "dp")),
        P(("expert", "dp"), None),
    )
    out_specs = P(("groups", "expert", "dp"), None)
    return jax.shard_map(local, mesh=mesh, in_specs=in_specs, out_specs=out_specs, check_vma=False)
```
